32 devices in a mesh: lat: 4 (over x, core), lon: 2 (over y), ch: 4 (over z).
Axes of the slice: x: 2, y: 2, z: 4, core: 2. Of those that a mesh axis runs over, the one named last changes fastest.
Arguments:
- grid_field: bfloat16 [1440, 4, 49152], P('lon', 'ch', 'lat'), may hold values from -6 to 6
- first_weight: bfloat16 [4, 2, 96, 96], P('ch'), may hold values from -0.4375 to 0.4375
- first_bias: float32 [4, 2, 96], P('ch'), may hold values from -3 to 3
- second_weight: bfloat16 [4, 2, 96, 96], P('ch'), may hold values from -0.4375 to 0.4375
- second_bias: float32 [4, 2, 96], P('ch'), may hold values from -3 to 3
Outputs:
- mixed: bfloat16 [1440, 4, 49152], P('lon', 'ch', 'lat')
The draws below stay inside these ranges and needn't reach their ends.
All inputs are finite; a program needn't handle non-finite values.
Results may differ from the reference program's by a relative error of at most 0.0073.
Values may be sent and summed in bfloat16 or wider, within the bound.
A program may use at most 256 MiB of HBM per device.

```python
import math
import jax
import jax.numpy as jnp
from jax import lax

H = 512
W = 1440
NB = 4
CB = 96


def level_of(stream_key, extent, pieces, least, high):
    level, own = 1.0, jax.random.fold_in(stream_key, 6)
    for dim, parts in pieces:
        steps = jnp.exp(jax.random.uniform(jax.random.fold_in(own, dim), (parts,), jnp.float32, least / len(pieces), high / len(pieces)))
        level = level * jnp.repeat(steps, extent[dim] // parts).reshape([-1 if axis == dim else 1 for axis in range(len(extent))])
    return level


def scatter_about(key, shape, spread, most, cuts=(), kind=jnp.bfloat16):
    gain = level_of(key, shape, cuts, -0.22, 0.18) if cuts else 1.0
    drawn = jax.random.normal(key, shape, jnp.float32) * spread * gain
    return jnp.minimum(jnp.maximum(drawn, -most), most).astype(kind)


def setup_inputs(seed: int = 0) -> dict:
    streams_of = jax.random.split(jax.random.key(seed), 6)
    return {
        "grid_field": scatter_about(streams_of[0], (W, NB, H * CB), 1.0, 6.0, ((0, 2), (1, 4), (2, 4))),
        "first_weight": scatter_about(streams_of[1], (NB, 2, CB, CB), (2 * CB) ** -0.5, 0.4375, ((0, 4),)),
        "first_bias": scatter_about(streams_of[2], (NB, 2, CB), 0.5, 3.0, ((0, 4),), jnp.float32),
        "second_weight": scatter_about(streams_of[3], (NB, 2, CB, CB), (2 * CB) ** -0.5, 0.4375, ((0, 4),)),
        "second_bias": scatter_about(streams_of[4], (NB, 2, CB), 0.5, 3.0, ((0, 4),), jnp.float32),
    }


shrink_level = 0.01

def phase_tables(length):
    indices = jnp.arange(length, dtype=jnp.int32)
    product = indices[:, None] * indices[None, :] % length
    angles = product.astype(jnp.float32) * (2.0 * math.pi / length)
    return (jnp.cos(angles), jnp.sin(angles))

def lon_tables(length):
    cosine_tab, sine_tab = phase_tables(length)
    kept_modes = length // 2
    factor = 1.0 / math.sqrt(length)
    forward = jnp.concatenate([cosine_tab[:kept_modes], -sine_tab[:kept_modes]], axis=0) * factor
    weights = jnp.where(jnp.arange(kept_modes) == 0, 1.0, 2.0).astype(jnp.float32)
    inverse = jnp.concatenate([cosine_tab[:, :kept_modes] * weights, -sine_tab[:, :kept_modes] * weights], axis=1) * factor
    return (forward.astype(jnp.bfloat16), inverse.astype(jnp.bfloat16))

def lat_tables(length):
    cosine_tab, sine_tab = phase_tables(length)
    factor = 1.0 / math.sqrt(length)
    forward = jnp.stack([jnp.stack([cosine_tab, sine_tab], axis=1), jnp.stack([-sine_tab, cosine_tab], axis=1)], axis=0) * factor
    inverse = jnp.stack([jnp.stack([cosine_tab, -sine_tab], axis=1), jnp.stack([sine_tab, cosine_tab], axis=1)], axis=0) * factor
    return (forward.astype(jnp.bfloat16), inverse.astype(jnp.bfloat16))

def complex_weight(weight):
    real_part, imag_part = (weight[0], weight[1])
    return jnp.stack([jnp.stack([real_part, imag_part], axis=1), jnp.stack([-imag_part, real_part], axis=1)], axis=0)

def block_mixing(mode_data, weight_one, bias_one, weight_two, bias_two):
    hidden = jnp.einsum('rkqc,rcsd->skqd', mode_data.astype(jnp.float32), complex_weight(weight_one).astype(jnp.float32), precision=lax.Precision.HIGHEST)
    hidden = jax.nn.relu(hidden + bias_one[:, None, None, :]).astype(jnp.bfloat16)
    output = jnp.einsum('rkqc,rcsd->skqd', hidden.astype(jnp.float32), complex_weight(weight_two).astype(jnp.float32), precision=lax.Precision.HIGHEST)
    output = output + bias_two[:, None, None, :]
    shrunk = jnp.sign(output) * jnp.maximum(jnp.abs(output) - shrink_level, 0.0)
    return shrunk.astype(jnp.bfloat16)

def reference(grid_field, first_weight, first_bias, second_weight, second_bias):
    kept_modes = W // 2
    lon_forward, lon_inverse = lon_tables(W)
    lat_forward, lat_inverse = lat_tables(H)
    lat_forward32 = lat_forward.astype(jnp.float32)
    lat_inverse32 = lat_inverse.astype(jnp.float32)
    blocks = jnp.moveaxis(grid_field, 1, 0)

    def per_block(inputs):
        block_field, weight_one, bias_one, weight_two, bias_two = inputs
        columns = block_field.reshape(W, H * CB)
        spectra = jnp.dot(lon_forward, columns, preferred_element_type=jnp.float32).astype(jnp.bfloat16)
        spectra = spectra.reshape(2, kept_modes, H, CB)
        mode_data = jnp.einsum('sqrh,rkhc->skqc', lat_forward32, spectra.astype(jnp.float32), precision=lax.Precision.HIGHEST).astype(jnp.bfloat16)
        shrunk = block_mixing(mode_data, weight_one, bias_one, weight_two, bias_two)
        returned = jnp.einsum('sqrh,rkhc->skqc', lat_inverse32, shrunk.astype(jnp.float32), precision=lax.Precision.HIGHEST).astype(jnp.bfloat16)
        grid_out = jnp.dot(lon_inverse, returned.reshape(2 * kept_modes, H * CB), preferred_element_type=jnp.float32) + columns.astype(jnp.float32)
        return grid_out.astype(jnp.bfloat16)
    mixed = lax.map(per_block, (blocks, first_weight, first_bias, second_weight, second_bias))
    return jnp.moveaxis(mixed, 0, 1)
```

```python
import math

import jax
import jax.numpy as jnp
import ml_dtypes
import numpy as np
from jax import lax
from jax.sharding import PartitionSpec as P

shrink_level = 0.01
row_chunks = 2
mode_chunks = 2
group = ("lat", "lon")


def phase_tables(length):
    indices = np.arange(length, dtype=np.int64)
    product = indices[:, None] * indices[None, :] % length
    angles = product.astype(np.float32) * np.float32(2.0 * math.pi / length)
    return np.cos(angles), np.sin(angles)


def chunk_sizes(modes):
    fours = -(-modes // 4)
    parts = min(mode_chunks, fours)
    return [4 * (fours * (i + 1) // parts - fours * i // parts) for i in range(parts)]


def lon_tables(length, owners, sizes, modes, lon_devices):
    cosine, sine = phase_tables(length)
    kept = length // 2
    local = length // lon_devices
    factor = np.float32(1.0 / math.sqrt(length))
    weights = np.where(np.arange(kept) == 0, 1.0, 2.0).astype(np.float32)[:, None]
    forward = np.stack([cosine[:kept], -sine[:kept]]) * factor
    inverse = np.stack([cosine[:kept] * weights, -sine[:kept] * weights]) * factor
    result = []
    start = 0
    for size in sizes:
        both = []
        for table in (forward, inverse):
            rows = np.zeros((owners, 2, size, length), np.float32)
            for owner in range(owners):
                low = owner * modes + start
                high = min(low + size, (owner + 1) * modes, kept)
                if high > low:
                    rows[owner, :, : high - low] = table[:, low:high]
            both.append(rows.reshape(owners, 2 * size, lon_devices, local))
        result.append(
            (
                both[0].transpose(0, 2, 1, 3).astype(ml_dtypes.bfloat16),
                both[1].transpose(2, 0, 3, 1).astype(ml_dtypes.bfloat16),
            )
        )
        start += size
    return result


def lat_tables(length):
    cosine, sine = phase_tables(length)
    factor = np.float32(1.0 / math.sqrt(length))
    forward = np.stack([np.stack([cosine, sine], 1), np.stack([-sine, cosine], 1)], 0) * factor
    inverse = np.stack([np.stack([cosine, -sine], 1), np.stack([sine, cosine], 1)], 0) * factor
    return forward.astype(ml_dtypes.bfloat16), inverse.astype(ml_dtypes.bfloat16)


def complex_blocks(weight):
    real_part, imag_part = (weight[:, 0], weight[:, 1])
    return jnp.stack(
        [jnp.stack([real_part, imag_part], axis=2), jnp.stack([-imag_part, real_part], axis=2)],
        axis=1,
    )


def block_mixing(mode_data, first_weight, first_bias, second_weight, second_bias):
    shape = mode_data.shape
    blocks_here = first_weight.shape[0]
    block_width = first_weight.shape[2]
    split_data = mode_data.reshape(shape[0], shape[1], shape[2], blocks_here, block_width)
    hidden = jnp.einsum(
        "rkqbc,brcsd->skqbd",
        split_data,
        complex_blocks(first_weight),
        preferred_element_type=jnp.float32,
    )
    hidden = jax.nn.relu(hidden + jnp.moveaxis(first_bias, 1, 0)[:, None, None, :, :]).astype(
        jnp.bfloat16
    )
    output = jnp.einsum(
        "rkqbc,brcsd->skqbd",
        hidden,
        complex_blocks(second_weight),
        preferred_element_type=jnp.float32,
    )
    output = output + jnp.moveaxis(second_bias, 1, 0)[:, None, None, :, :]
    shrunk = jnp.sign(output) * jnp.maximum(jnp.abs(output) - shrink_level, 0.0)
    return shrunk.astype(jnp.bfloat16).reshape(shape)


def partner_permute(value, axes, count, step):
    return lax.ppermute(value, axes, [(i, i ^ step) for i in range(count)])


def per_device(grid_field, first_weight, first_bias, second_weight, second_bias):
    lon_devices = lax.axis_size("lon")
    lat_devices = lax.axis_size("lat")
    owners = lon_devices * lat_devices
    block_width = first_weight.shape[2]
    local_lon, blocks_here, merged = grid_field.shape
    local_lat = merged // block_width
    lon_size = local_lon * lon_devices
    lat_size = local_lat * lat_devices
    modes = -(-(lon_size // 2) // owners)
    sizes = chunk_sizes(modes)
    lon_chunks = lon_tables(lon_size, owners, sizes, modes, lon_devices)
    lat_forward, lat_inverse = lat_tables(lat_size)

    assert blocks_here == 1
    lon_index = lax.axis_index("lon")
    me = lax.axis_index("lat") * lon_devices + lon_index
    pairwise = owners <= 8 and owners & (owners - 1) == 0
    order = [(me ^ s) if pairwise else s for s in range(owners)]
    lon_order = [lon_index ^ t for t in range(lon_devices)]

    def exchange(pieces):
        if pairwise:
            return [
                partner_permute(piece, group, owners, s) if s else piece
                for s, piece in enumerate(pieces)
            ]
        joined = lax.all_to_all(
            jnp.concatenate(pieces, axis=0), group, split_axis=0, concat_axis=0, tiled=True
        )
        return jnp.split(joined, owners, axis=0)

    own_rows = local_lat // lon_devices
    own_columns = own_rows * block_width
    chunk_columns = own_columns // row_chunks
    flat = grid_field.reshape(local_lon, merged)

    def field_piece(owner, chunk):
        return lax.dynamic_slice(
            flat, (0, owner * own_columns + chunk * chunk_columns), (local_lon, chunk_columns)
        )

    gathered = []
    for c in range(row_chunks):
        pieces = [
            partner_permute(field_piece(lon_order[t], c), "lon", lon_devices, t)
            if t
            else field_piece(lon_index, c)
            for t in range(lon_devices)
        ]
        gathered.append(jnp.concatenate(pieces, axis=0))

    def pick(table, indices, axis):
        table = jnp.asarray(table)
        return [lax.dynamic_index_in_dim(table, i, axis, keepdims=False) for i in indices]

    forward_tables = []
    inverse_tables = []
    for forward, inverse in lon_chunks:
        rows = jnp.concatenate(pick(forward, order, 0), axis=1)
        forward_tables.append(jnp.concatenate(pick(rows, lon_order, 0), axis=1))
        halves = pick(inverse, lon_order, 0)
        inverse_tables.append([jnp.concatenate(pick(half, order, 0), axis=1) for half in halves])
    inverse_tables = [
        jnp.concatenate([chunk[t] for chunk in inverse_tables], axis=1) for t in range(lon_devices)
    ]

    def row_blocks(table, axis):
        table = jnp.asarray(table)
        return jnp.concatenate(
            [lax.dynamic_slice_in_dim(table, i * own_rows, own_rows, axis) for i in order],
            axis=axis,
        )

    lat_forward = row_blocks(lat_forward, 3)
    lat_inverse = row_blocks(lat_inverse, 1)

    returned_pieces = []
    for size, table in zip(sizes, forward_tables):
        received = []
        for c in range(row_chunks):
            spectra = jnp.dot(table, gathered[c], preferred_element_type=jnp.float32).astype(
                jnp.bfloat16
            )
            received.append(exchange(jnp.split(spectra, owners, axis=0)))
        data = jnp.concatenate(
            [received[c][s] for s in range(owners) for c in range(row_chunks)], axis=1
        )
        data = data.reshape(2, size, lat_size, block_width)
        mode_data = jnp.einsum(
            "sqrh,rkhc->skqc", lat_forward, data, preferred_element_type=jnp.float32
        ).astype(jnp.bfloat16)
        shrunk = block_mixing(mode_data, first_weight, first_bias, second_weight, second_bias)
        returned = jnp.einsum(
            "shrq,rkqc->skhc", lat_inverse, shrunk, preferred_element_type=jnp.float32
        ).astype(jnp.bfloat16)
        returned = returned.reshape(2 * size, lat_size * block_width)
        by_chunk = []
        for c in range(row_chunks):
            starts = [s * own_columns + c * chunk_columns for s in range(owners)]
            by_chunk.append(exchange([returned[:, a : a + chunk_columns] for a in starts]))
        returned_pieces.append(by_chunk)

    out = jnp.zeros((local_lon, merged), jnp.bfloat16)
    for c in range(row_chunks):
        columns = jnp.concatenate(
            [piece for by_chunk in returned_pieces for piece in by_chunk[c]], axis=0
        )
        for t in reversed(range(lon_devices)):
            field_rows = gathered[c][t * local_lon : (t + 1) * local_lon]
            mixed = jnp.dot(inverse_tables[t], columns, preferred_element_type=jnp.float32)
            mixed = (mixed + field_rows.astype(jnp.float32)).astype(jnp.bfloat16)
            if t:
                mixed = partner_permute(mixed, "lon", lon_devices, t)
            start = lon_order[t] * own_columns + c * chunk_columns
            out = lax.dynamic_update_slice(out, mixed, (0, start))
    return out.reshape(grid_field.shape)


def solution(mesh):
    in_specs = (
        P("lon", "ch", "lat"),
        P("ch", None, None, None),
        P("ch", None, None),
        P("ch", None, None, None),
        P("ch", None, None),
    )
    out_specs = P("lon", "ch", "lat")
    return jax.shard_map(
        per_device, mesh=mesh, in_specs=in_specs, out_specs=out_specs, check_vma=False
    )
```
